128 devices in a mesh: col: 4 (over x), row: 32 (over z, y, core).
Axes of the slice: x: 4, y: 4, z: 4, core: 2. Of those that a mesh axis runs over, the one named last changes fastest.
Arguments:
- velocity: bfloat16 [4, 2097152], P(None, ('col', 'row')), may hold values from -6 to 6
- pair_struct: int32 [16384], P(('col', 'row')), may hold values from 0 to 63
- pair_panel: int32 [16384], P(('col', 'row')), may hold values from 0 to 127
- pair_count: int32 [128], P(('col', 'row')), may hold values from 32 to 128, as said below
- mortar_coef: bfloat16 [16384, 128, 128], P(('col', 'row')), may hold values from -0.0625 to 0.0625
- bem_matrix: bfloat16 [32768, 32768], P('row', 'col'), may hold values from -0.03125 to 0.03125
- self_term: float32 [32768], P('row'), may hold values from 0.5 to 2
Outputs:
- pressure: bfloat16 [4, 32768], P(None, 'row')
- load: float32 [4, 2097152], P(None, ('col', 'row'))
The draws below stay inside these ranges and needn't reach their ends.
Inputs may be any that keep to these rules, and one draw needn't show every extreme that they name: pair_struct numbers a structural block within the slot's own device. `pair_count`: some device has all its slots live.
All inputs are finite; a program needn't handle non-finite values.
Results may differ from the reference program's by a relative error of at most 0.005.
Values may be sent and summed in bfloat16 or wider, within the bound.
A program may use at most 128 MiB of HBM per device.

```python
import math
import jax
import jax.numpy as jnp
import numpy as np
from jax import lax

BLK = 128
PANELS = 16384
LOADS = 4
PAIRS_DEV = 128
NBLK = 128
SBLK_DEV = 64
NODES = 1048576
SLOTS = 16384
N_COL = 4
N_ROW = 32


def draw_pair_count(key, part):
    key_counts = jax.random.fold_in(key, 11)
    key_full = jax.random.fold_in(key, 12)
    counts = jax.random.randint(key_counts, (N_COL * N_ROW,), PAIRS_DEV // 4, PAIRS_DEV + 1)
    chosen = jax.random.randint(key_full, (), 0, N_COL * N_ROW)
    return jnp.where(jnp.arange(N_COL * N_ROW) == chosen, PAIRS_DEV, counts).astype(jnp.int32)


def plant(drawn, key, smallest, largest):
    longest = drawn.shape.index(max(drawn.shape))
    spots = []
    for shift in (0, 1):
        where = [jax.random.randint(jax.random.fold_in(key, axis), (), 0, length) for axis, length in enumerate(drawn.shape)]
        where[longest] = (where[longest] + shift) % drawn.shape[longest]
        spots.append(tuple(where))
    return drawn.at[spots[0]].set(smallest).at[spots[1]].set(largest)


def steps_of(stream_key, extent, cuts, smallest, top_value):
    def one(dim, parts):
        draws = jax.random.uniform(jax.random.fold_in(jax.random.fold_in(stream_key, 6), dim), (parts,), jnp.float32, smallest / len(cuts), top_value / len(cuts))
        return jnp.repeat(jnp.exp(draws), extent[dim] // parts).reshape((-1,) + (1,) * (len(extent) - dim - 1))

    level = one(*cuts[0])
    for cut in cuts[1:]:
        level = level * one(*cut)
    return level


def rank_table(count, skew):
    portions = [(1 << 20) // math.isqrt(rank ** skew) + 1 for rank in range(1, count + 1)]
    scale = 1 + sum(portions) // (1 << 30)
    return np.cumsum(np.array([max(1, weight // scale) for weight in portions]))


def skewed_ids(stream_key, dims, amount, slope):
    grid = rank_table(amount, slope)
    ticket = jax.random.randint(jax.random.fold_in(stream_key, 1), dims, 0, int(grid[amount - 1]))
    standing = jnp.searchsorted(jnp.asarray(grid, jnp.int32), ticket, side="right")
    return jax.random.permutation(jax.random.fold_in(stream_key, 2), amount)[standing].astype(jnp.int32)


def gaussian(stream_key, extent, width, most, split=(), kind=jnp.bfloat16):
    loudness = steps_of(stream_key, extent, split, -0.22, 0.18) if split else 1.0
    array = jax.random.normal(stream_key, extent, jnp.float32) * width * loudness
    return jnp.minimum(jnp.maximum(array, -most), most).astype(kind)


def setup_inputs(seed: int = 0) -> dict:
    splits = jax.random.split(jax.random.key(seed), 8)
    velocity = gaussian(splits[0], (LOADS, 2 * NODES), 1.0, 6.0, ((1, 128),))
    pair_struct = plant(jax.random.randint(splits[1], (SLOTS,), 0, SBLK_DEV), jax.random.fold_in(splits[1], 1), 0, SBLK_DEV - 1).astype(jnp.int32)
    pair_panel = plant(skewed_ids(splits[2], (SLOTS,), NBLK, 2), jax.random.fold_in(splits[2], 3), 0, NBLK - 1).astype(jnp.int32)
    pair_count = draw_pair_count(jax.random.fold_in(splits[7], 71), 0)
    mortar_coef = gaussian(splits[4], (SLOTS, BLK, BLK), (BLK * PAIRS_DEV // 2) ** -0.5, 0.0625, ((0, 128),))
    bem_matrix = gaussian(splits[5], (2 * PANELS, 2 * PANELS), (2 * PANELS) ** -0.5, 0.03125, ((0, 32), (1, 4)))
    self_term = jnp.clip(jnp.exp(math.log(2.0) - 1.3862944 * jax.random.uniform(splits[6], (2 * PANELS,), jnp.float32) ** steps_of(splits[6], (2 * PANELS,), ((0, 32),), -0.2, 0.2)), 0.5, 2.0)
    return {"velocity": velocity, "pair_struct": pair_struct, "pair_panel": pair_panel, "pair_count": pair_count, "mortar_coef": mortar_coef, "bem_matrix": bem_matrix, "self_term": self_term}


def reference(velocity, pair_struct, pair_panel, pair_count, mortar_coef, bem_matrix, self_term):
    devcount = N_COL * N_ROW
    vel_dev = velocity.reshape(LOADS, devcount, SBLK_DEV, 2 * BLK).transpose(1, 0, 2, 3)
    coef_dev = mortar_coef.reshape(devcount, PAIRS_DEV, BLK, BLK)
    struct_dev = pair_struct.reshape(devcount, PAIRS_DEV)
    panel_dev = pair_panel.reshape(devcount, PAIRS_DEV)
    slot_ids = jnp.arange(PAIRS_DEV, dtype=jnp.int32)

    def forward(total, items):
        vel_one, coef_one, struct_one, panel_one, count_one = items
        live_mask = slot_ids < count_one
        picked = jnp.take(vel_one, struct_one, axis=1).reshape(LOADS, PAIRS_DEV, BLK, 2)
        terms = jnp.einsum("qpn,cqnk->cqpk", coef_one.astype(jnp.float32), picked.astype(jnp.float32), precision=lax.Precision.HIGHEST)
        onehot = ((panel_one[:, None] == jnp.arange(NBLK, dtype=jnp.int32)[None, :]) & live_mask[:, None]).astype(jnp.float32)
        return total + jnp.einsum("qb,cqpk->cbpk", onehot, terms, precision=lax.Precision.HIGHEST), None

    start = jnp.zeros((LOADS, NBLK, BLK, 2), jnp.float32)
    total, unused = lax.scan(forward, start, (vel_dev, coef_dev, struct_dev, panel_dev, pair_count))
    xvec = total.reshape(LOADS, 2 * PANELS).astype(jnp.bfloat16)
    pressure = jnp.dot(xvec, bem_matrix.T, preferred_element_type=jnp.float32)
    pressure = (pressure + self_term[None, :] * xvec.astype(jnp.float32)).astype(jnp.bfloat16)
    panel_view = pressure.reshape(LOADS, NBLK, 2 * BLK)

    def backward(carry, items):
        coef_one, struct_one, panel_one, count_one = items
        live_mask = slot_ids < count_one
        took = jnp.take(panel_view, panel_one, axis=1).reshape(LOADS, PAIRS_DEV, BLK, 2)
        terms = jnp.einsum("qpn,cqpk->cqnk", coef_one.astype(jnp.float32), took.astype(jnp.float32), precision=lax.Precision.HIGHEST)
        onehot = ((struct_one[:, None] == jnp.arange(SBLK_DEV, dtype=jnp.int32)[None, :]) & live_mask[:, None]).astype(jnp.float32)
        return carry, jnp.einsum("qs,cqnk->csnk", onehot, terms, precision=lax.Precision.HIGHEST)

    unused2, loads_dev = lax.scan(backward, jnp.zeros((), jnp.float32), (coef_dev, struct_dev, panel_dev, pair_count))
    load = loads_dev.transpose(1, 0, 2, 3, 4).reshape(LOADS, 2 * NODES)
    return pressure, load
```

```python
import functools

import jax
import jax.numpy as jnp
from jax import lax
from jax.experimental import pallas as pl
from jax.experimental.pallas import tpu as pltpu
from jax.sharding import PartitionSpec as P

NT = (((1,), (1,)), ((), ()))
NN = (((1,), (0,)), ((), ()))
MESH = pl.DeviceIdType.MESH
F32 = jnp.float32
BF16 = jnp.bfloat16
ROWS = 8
PER = 16
GIB = 1 << 30


def parting(width):
    src = lax.broadcasted_iota(jnp.int32, (width, width), 0)
    dst = lax.broadcasted_iota(jnp.int32, (width, width), 1)
    half = width // 2
    to = jnp.where(src % 2 == 1, half, 0) + src // 2
    return jnp.where(to == dst, 1.0, 0.0).astype(BF16)


def first_part(shape):
    return lax.broadcasted_iota(jnp.int32, shape, 0) % ROWS < ROWS // 2


def to_parts(rows, part):
    half = part.shape[0] // 2
    both = lax.dot_general(rows, part, NN, preferred_element_type=F32)
    keep = first_part((rows.shape[0], half))
    return jnp.where(keep, both[:, :half], both[:, half:])


def from_parts(rows, part):
    keep = first_part(rows.shape)
    zero = jnp.zeros_like(rows)
    wide = jnp.concatenate([jnp.where(keep, rows, zero), jnp.where(keep, zero, rows)], 1)
    return lax.dot_general(wide.astype(BF16), part, NT, preferred_element_type=F32)


def pair_products(source, take_ids, add_ids, count, coef_any, coef, sems, table, acc, dims):
    slots = coef.shape[0]
    chunks = slots // PER
    copies = [
        pltpu.make_async_copy(
            coef_any.at[pl.ds(i * PER, PER)], coef.at[pl.ds(i * PER, PER)], sems.at[i]
        )
        for i in range(chunks)
    ]
    for copy in copies:
        copy.start()
    source(table)
    acc[...] = jnp.zeros_like(acc)
    live = count[0]
    along = 1 if dims is NT else 0
    for i in range(chunks):
        copies[i].wait()

        def two(s, carry, i=i):
            q = i * PER + 2 * s
            a, b = table[take_ids[q]], table[take_ids[q + 1]]
            zero = jnp.zeros_like(a)
            left = jnp.concatenate(
                [jnp.concatenate([a, zero], 1), jnp.concatenate([zero, b], 1)], 0
            ).astype(BF16)
            right = jnp.concatenate([coef[q], coef[q + 1]], along)
            term = lax.dot_general(left, right, dims, preferred_element_type=F32)
            for k in range(2):
                where = add_ids[q + k]
                acc[where] = acc[where] + jnp.where(q + k < live, term[k * ROWS : (k + 1) * ROWS], 0.0)
            return carry

        lax.fori_loop(0, PER // 2, two, 0, unroll=PER // 2)


def forward_kernel(struct, panel, count, vel, coef_any, out, coef, sems, wide, table, acc):
    def source(table):
        vals = vel[...].astype(F32)
        both = jnp.concatenate([vals, vals], 0)
        blocks, _, width = wide.shape
        for b in range(blocks):
            wide[b] = both[:, b * width : (b + 1) * width]
        rows = wide[...].reshape(blocks * ROWS, width).astype(BF16)
        table[...] = to_parts(rows, parting(width)).reshape(table.shape)

    pair_products(source, struct, panel, count, coef_any, coef, sems, table, acc, NT)
    out[...] = acc[...].reshape(out.shape).astype(BF16)


def backward_kernel(struct, panel, count, press, coef_any, out, coef, sems, table, acc):
    def source(table):
        table[...] = press[...].astype(F32).reshape(table.shape)

    pair_products(source, panel, struct, count, coef_any, coef, sems, table, acc, NN)
    blocks, _, half = acc.shape
    part = parting(2 * half)
    rows = acc[...].reshape(blocks * ROWS, half)
    high = rows.astype(BF16).astype(F32)
    mixed = from_parts(high, part) + from_parts(rows - high, part)
    mixed = mixed.reshape(blocks, ROWS, 2 * half)
    cases = out.shape[0]
    for b in range(blocks):
        one = mixed[b]
        out[:, b * 2 * half : (b + 1) * 2 * half] = one[:cases] + one[cases:]


def field_kernel(
    nx, nz, nw, partial, bem_any, self_term, press, full,
    bem, got_x, sum_x, got_z, sum_z, got_w, mine, line, entries, terms,
    bem_sems, send, recv,
):
    col = lax.axis_index("col")
    row = lax.axis_index("row")
    z, w = row // nw, row % nw
    width = bem.shape[2] // nw
    half = width // 2
    own = press.shape[1] // width
    cases = press.shape[0]

    loads = [
        pltpu.make_async_copy(
            bem_any.at[:, pl.ds(i * nw * width, nw * width)], bem.at[i], bem_sems.at[i]
        )
        for i in range(nz)
    ]
    for load in loads:
        load.start()

    def along_x(d):
        return (lax.rem(col + d, nx), row)

    def along_z(d):
        return (col, lax.rem(z + d, nz) * nw + w)

    def along_w(d):
        return (col, z * nw + lax.rem(w + d, nw))

    xs, zs, ws = range(1, nx), range(1, nz), range(1, nw)
    friends = [along_x(d) for d in xs] + [along_z(d) for d in zs] + [along_w(d) for d in ws]
    barrier = pltpu.get_barrier_semaphore()
    for friend in friends:
        pl.semaphore_signal(barrier, inc=1, device_id=friend, device_id_type=MESH)
    pl.semaphore_wait(barrier, len(friends))

    started = []

    def go(src, dst, device):
        i = len(started)
        copy = pltpu.make_async_remote_copy(
            src_ref=src, dst_ref=dst, send_sem=send.at[i], recv_sem=recv.at[i],
            device_id=device, device_id_type=MESH,
        )
        copy.start()
        started.append(copy)
        return copy

    def rows_of(index, count):
        return pl.ds(pl.multiple_of(index * count, count), count)

    n_x = sum_x.shape[0]
    copies = [
        go(partial.at[rows_of(lax.rem(col + d, nx), n_x)], got_x.at[d - 1], along_x(d)) for d in xs
    ]
    total = partial[rows_of(col, n_x), :].astype(F32)
    for d in xs:
        copies[d - 1].wait_recv()
        total = total + got_x[d - 1].astype(F32)
    sum_x[...] = total

    n_z = sum_z.shape[0]
    copies = [
        go(sum_x.at[rows_of(lax.rem(z + d, nz), n_z)], got_z.at[d - 1], along_z(d)) for d in zs
    ]
    total = sum_x[rows_of(z, n_z), :]
    for d in zs:
        copies[d - 1].wait_recv()
        total = total + got_z[d - 1]
    sum_z[...] = total

    copies = [
        go(sum_z.at[rows_of(lax.rem(w + d, nw), ROWS)], got_w.at[d - 1], along_w(d)) for d in ws
    ]
    total = sum_z[rows_of(w, ROWS), :]
    for d in ws:
        copies[d - 1].wait_recv()
        total = total + got_w[d - 1]
    mine[rows_of(w, ROWS), :] = total.astype(BF16).astype(F32)

    copies = [go(mine.at[rows_of(w, ROWS)], mine.at[rows_of(w, ROWS)], along_w(d)) for d in ws]
    for copy in copies:
        copy.wait_recv()
    line[z] = mine[...].astype(BF16)
    copies = [go(line.at[z], line.at[z], along_z(d)) for d in zs]
    for load in loads:
        load.wait()
    part = parting(width)
    sums = jnp.zeros((ROWS, press.shape[1]), F32)
    for d in [0, *zs]:
        if d:
            copies[d - 1].wait_recv()
        at = lax.rem(z + nz - d, nz)
        lhs = from_parts(line[at].astype(F32), part)
        entries[pl.ds(at * nw, nw)] = lhs.reshape(nw, ROWS, width)
        lhs = lhs.astype(BF16)
        long = jnp.concatenate([lhs[j * ROWS : (j + 1) * ROWS] for j in range(nw)], 1)
        sums = sums + lax.dot_general(long, bem[at], NT, preferred_element_type=F32)
    first = row * own
    blocks = nz * nw
    owner = first // blocks == col
    here = lax.rem(first, blocks)
    same = jnp.concatenate([entries[here + u] for u in range(own)], 1)
    sums = sums + jnp.where(owner, same * self_term[...], 0.0)
    terms[col] = sums[:cases] + sums[cases:]

    copies = [go(terms.at[col], terms.at[col], along_x(d)) for d in xs]
    for copy in copies:
        copy.wait_recv()
    total = terms[0]
    for j in range(1, nx):
        total = total + terms[j]
    rounded = total.astype(BF16)
    press[...] = rounded
    wide = rounded.astype(F32)
    wide = jnp.concatenate([wide, wide], 0)
    wide = jnp.concatenate([wide[:, u * width : (u + 1) * width] for u in range(own)], 0)
    n_own = own * ROWS
    full[rows_of(row, n_own), :] = to_parts(wide.astype(BF16), part).astype(BF16)

    copies = [go(full.at[rows_of(row, n_own)], full.at[rows_of(row, n_own)], along_w(d)) for d in ws]
    for copy in copies:
        copy.wait_recv()
    n_line = n_own * nw
    copies = [go(full.at[rows_of(z, n_line)], full.at[rows_of(z, n_line)], along_z(d)) for d in zs]
    for copy in copies:
        copy.wait_recv()
    for copy in started:
        copy.wait_send()


def on_device(nx, nz, nw, velocity, pair_struct, pair_panel, pair_count, mortar_coef, bem_matrix, self_term):
    cases = velocity.shape[0]
    slots, panel_size, node_size = mortar_coef.shape
    node_blocks = velocity.shape[1] // (2 * node_size)
    width = 2 * panel_size
    col_blocks = bem_matrix.shape[1] // width
    panel_blocks = nx * col_blocks
    press_rows = bem_matrix.shape[0]
    own = press_rows // width
    smem = pl.BlockSpec(memory_space=pltpu.SMEM)
    vmem = pl.BlockSpec(memory_space=pltpu.VMEM)
    hbm = pl.BlockSpec(memory_space=pl.ANY)
    mortar_cost = pl.CostEstimate(
        flops=2 * ROWS * mortar_coef.size, bytes_accessed=2 * mortar_coef.size, transcendentals=0
    )
    coef_scratch = [
        pltpu.VMEM(mortar_coef.shape, BF16),
        pltpu.SemaphoreType.DMA((slots // PER,)),
    ]
    partial = pl.pallas_call(
        forward_kernel,
        out_shape=jax.ShapeDtypeStruct((panel_blocks * ROWS, panel_size), BF16),
        in_specs=[smem, smem, smem, vmem, hbm],
        out_specs=vmem,
        scratch_shapes=coef_scratch
        + [
            pltpu.VMEM((node_blocks, ROWS, 2 * node_size), F32),
            pltpu.VMEM((node_blocks, ROWS, node_size), F32),
            pltpu.VMEM((panel_blocks, ROWS, panel_size), F32),
        ],
        compiler_params=pltpu.CompilerParams(vmem_limit_bytes=24 << 20),
        cost_estimate=mortar_cost,
        name="mortar_forward",
    )(pair_struct, pair_panel, pair_count, velocity, mortar_coef)

    sends = 2 * (nx - 1) + 3 * (nz - 1) + 3 * (nw - 1)
    pressure, full = pl.pallas_call(
        functools.partial(field_kernel, nx, nz, nw),
        out_shape=(
            jax.ShapeDtypeStruct((cases, press_rows), BF16),
            jax.ShapeDtypeStruct((panel_blocks * ROWS, panel_size), BF16),
        ),
        in_specs=[vmem, hbm, vmem],
        out_specs=(vmem, vmem),
        scratch_shapes=[
            pltpu.VMEM((nz, press_rows, nw * width), BF16),
            pltpu.VMEM((nx - 1, col_blocks * ROWS, panel_size), BF16),
            pltpu.VMEM((col_blocks * ROWS, panel_size), F32),
            pltpu.VMEM((nz - 1, nw * ROWS, panel_size), F32),
            pltpu.VMEM((nw * ROWS, panel_size), F32),
            pltpu.VMEM((nw - 1, ROWS, panel_size), F32),
            pltpu.VMEM((nw * ROWS, panel_size), F32),
            pltpu.VMEM((nz, nw * ROWS, panel_size), BF16),
            pltpu.VMEM((nz * nw, ROWS, width), F32),
            pltpu.VMEM((nx, cases, press_rows), F32),
            pltpu.SemaphoreType.DMA((nz,)),
            pltpu.SemaphoreType.DMA((sends,)),
            pltpu.SemaphoreType.DMA((sends,)),
        ],
        compiler_params=pltpu.CompilerParams(
            collective_id=0, has_side_effects=True, vmem_limit_bytes=48 << 20
        ),
        cost_estimate=pl.CostEstimate(
            flops=2 * cases * bem_matrix.size,
            bytes_accessed=2 * bem_matrix.size,
            transcendentals=0,
        ),
        name="field",
    )(partial, bem_matrix, self_term[None, :])

    load = pl.pallas_call(
        backward_kernel,
        out_shape=jax.ShapeDtypeStruct(velocity.shape, F32),
        in_specs=[smem, smem, smem, vmem, hbm],
        out_specs=vmem,
        scratch_shapes=coef_scratch
        + [
            pltpu.VMEM((panel_blocks, ROWS, panel_size), F32),
            pltpu.VMEM((node_blocks, ROWS, node_size), F32),
        ],
        compiler_params=pltpu.CompilerParams(vmem_limit_bytes=24 << 20),
        cost_estimate=mortar_cost,
        name="mortar_backward",
    )(pair_struct, pair_panel, pair_count, full, mortar_coef)
    return pressure, load


def solution(mesh):
    nx = mesh.shape["col"]
    rows = mesh.shape["row"]
    nz = nx if rows % nx == 0 else 1
    placed = (
        P(None, ("col", "row")),
        P(("col", "row")),
        P(("col", "row")),
        P(("col", "row")),
        P(("col", "row"), None, None),
        P("row", "col"),
        P("row"),
    )
    return jax.shard_map(
        functools.partial(on_device, nx, nz, rows // nz),
        mesh=mesh,
        in_specs=placed,
        out_specs=(P(None, "row"), P(None, ("col", "row"))),
        check_vma=False,
    )
```

```python
import functools

import jax
import jax.numpy as jnp
from jax import lax
from jax.experimental import pallas as pl
from jax.experimental.pallas import tpu as pltpu
from jax.sharding import PartitionSpec as P

NT = (((1,), (1,)), ((), ()))
NN = (((1,), (0,)), ((), ()))
MESH = pl.DeviceIdType.MESH
F32 = jnp.float32
BF16 = jnp.bfloat16
ROWS = 8
PER = 16
CORES = 2
LAG = 6


def parting(width):
    src = lax.broadcasted_iota(jnp.int32, (width, width), 0)
    dst = lax.broadcasted_iota(jnp.int32, (width, width), 1)
    half = width // 2
    to = jnp.where(src % 2 == 1, half, 0) + src // 2
    return jnp.where(to == dst, 1.0, 0.0).astype(BF16)


def first_part(shape):
    return lax.broadcasted_iota(jnp.int32, shape, 0) % ROWS < ROWS // 2


def to_parts(rows, part):
    half = part.shape[0] // 2
    both = lax.dot_general(rows, part, NN, preferred_element_type=F32)
    keep = first_part((rows.shape[0], half))
    return jnp.where(keep, both[:, :half], both[:, half:])


def from_parts(rows, part):
    keep = first_part(rows.shape)
    zero = jnp.zeros_like(rows)
    wide = jnp.concatenate([jnp.where(keep, rows, zero), jnp.where(keep, zero, rows)], 1)
    return lax.dot_general(wide.astype(BF16), part, NT, preferred_element_type=F32)


def pair_term(table, ids, coef, q, dims):
    a, b = table[ids(q)], table[ids(q + 1)]
    zero = jnp.zeros_like(a)
    left = jnp.concatenate(
        [jnp.concatenate([a, zero], 1), jnp.concatenate([zero, b], 1)], 0
    ).astype(BF16)
    right = jnp.concatenate([coef[q], coef[q + 1]], 1 if dims is NT else 0)
    return lax.dot_general(left, right, dims, preferred_element_type=F32)


def backward_kernel(struct, panel, count, press, full, coef, out, press_out, table, acc):
    press_out[...] = press[...]
    table[...] = full[...].astype(F32).reshape(table.shape)
    acc[...] = jnp.zeros_like(acc)
    live = count[0, 0]

    def two(s, carry):
        q = 2 * s
        term = pair_term(table, lambda i: panel[0, i], coef, q, NN)
        for k in range(2):
            where = struct[0, q + k]
            acc[where] = acc[where] + jnp.where(q + k < live, term[k * ROWS : (k + 1) * ROWS], 0.0)
        return carry

    lax.fori_loop(0, coef.shape[0] // 2, two, 0, unroll=PER // 2)
    blocks, _, half = acc.shape
    part = parting(2 * half)
    rows = acc[...].reshape(blocks * ROWS, half)
    high = rows.astype(BF16).astype(F32)
    mixed = from_parts(high, part) + from_parts(rows - high, part)
    mixed = mixed.reshape(blocks, ROWS, 2 * half)
    cases = out.shape[0]
    for b in range(blocks):
        one = mixed[b]
        out[:, b * 2 * half : (b + 1) * 2 * half] = one[:cases] + one[cases:]


def field_kernel(
    nx, nz, ny, count, struct_any, panel_any, vel_any, coef_any, bem_any, self_any,
    press, full,
    struct, panel, panel_row, vel, coef, bem, self_term, wide, table, pair_rows,
    sums_all, got_core, half_16, got_zy, sum_zy, got_x, line, terms,
    in_sems, coef_sems, bem_sems, send, recv,
):
    col = lax.axis_index("col")
    row = lax.axis_index("row")
    chip, core = row // CORES, row % CORES
    z, y = chip // ny, chip % ny
    chips = nz * ny
    slots, size, _ = coef.shape
    width = 2 * size
    cases, press_rows = press.shape
    own = press_rows // width

    small = [
        (struct_any, struct), (panel_any, panel),
        (panel_any, panel_row), (vel_any, vel), (self_any, self_term),
    ]
    ins = [pltpu.make_async_copy(a, b, in_sems.at[i]) for i, (a, b) in enumerate(small)]
    coefs = [
        pltpu.make_async_copy(
            coef_any.at[pl.ds(i * PER, PER)], coef.at[pl.ds(i * PER, PER)], coef_sems.at[i]
        )
        for i in range(slots // PER)
    ]
    wide_chip = CORES * width
    loads = [
        pltpu.make_async_copy(
            bem_any.at[:, pl.ds(i * wide_chip, wide_chip)], bem.at[i], bem_sems.at[i]
        )
        for i in range(chips)
    ]
    for copy in [*ins, *coefs]:
        copy.start()

    def at_x(d):
        return (lax.rem(col + d, nx), row)

    def chip_at(dz, dy):
        return lax.rem(z + dz + nz, nz) * ny + lax.rem(y + dy + ny, ny)

    def at_zy(step):
        return (col, chip_at(*step) * CORES + core)

    def hops(step):
        return min(step[0], nz - step[0]) + min(step[1], ny - step[1])

    sibling = (col, chip * CORES + 1 - core)
    xs = range(1, nx)
    near = sorted([(a, b) for a in range(nz) for b in range(ny) if a or b], key=hops)
    friends = [at_zy(s) for s in near[::-1]] + [at_x(d) for d in xs] + [sibling]
    barrier = pltpu.get_barrier_semaphore()
    for friend in friends:
        pl.semaphore_signal(barrier, inc=1, device_id=friend, device_id_type=MESH)

    started = []

    def go(src, dst, device):
        i = len(started)
        copy = pltpu.make_async_remote_copy(
            src_ref=src, dst_ref=dst, send_sem=send.at[i], recv_sem=recv.at[i],
            device_id=device, device_id_type=MESH,
        )
        copy.start()
        started.append(copy)
        return copy

    def rows_of(index, n):
        return pl.ds(pl.multiple_of(index * n, n), n)

    part = parting(width)
    for copy in ins:
        copy.wait()
    vals = vel[...].astype(F32)
    both = jnp.concatenate([vals, vals], 0)
    node_blocks = wide.shape[0]
    for b in range(node_blocks):
        wide[b] = both[:, b * width : (b + 1) * width]
    table[...] = to_parts(
        wide[...].reshape(node_blocks * ROWS, width).astype(BF16), part
    ).reshape(table.shape)
    for i in range(slots // PER):
        coefs[i].wait()
        if i == slots // PER - 1:
            for load in loads:
                load.start()

        def two(s, carry, i=i):
            q = i * PER + 2 * s
            term = pair_term(table, lambda j: struct[0, j], coef, q, NT)
            pair_rows[pl.ds(pl.multiple_of(q * ROWS, 2 * ROWS), 2 * ROWS), :] = term
            return carry

        lax.fori_loop(0, PER // 2, two, 0, unroll=PER // 2)

    panel_blocks = nx * chips * CORES
    place = lax.broadcasted_iota(jnp.int32, (panel_blocks, slots), 0)
    block = (place % nx) * (chips * CORES) + (place // nx) % chips * CORES + place // (nx * chips)
    slot = lax.broadcasted_iota(jnp.int32, (panel_blocks, slots), 1)
    hit = (panel_row[...] == block) & (slot < count[0, 0])
    hit = jnp.where(hit, 1.0, 0.0).astype(BF16)
    hit = jnp.concatenate([hit, hit], 1)
    for r in range(ROWS):
        term = pair_rows[pl.ds(r, slots, stride=ROWS), :]
        high = term.astype(BF16)
        low = (term - high.astype(F32)).astype(BF16)
        sums_all[pl.ds(r, panel_blocks, stride=ROWS), :] = lax.dot_general(
            hit, jnp.concatenate([high, low], 0), NN, preferred_element_type=F32
        )

    pl.semaphore_wait(barrier, len(friends))

    n_core = got_core.shape[0]
    copy = go(sums_all.at[rows_of(1 - core, n_core)], got_core, sibling)
    copy.wait_recv()
    half_16[...] = (sums_all[rows_of(core, n_core), :] + got_core[...]).astype(BF16)

    n_zy = nx * ROWS
    copies = {
        s: go(half_16.at[rows_of(chip_at(*s), n_zy)], got_zy.at[k], at_zy(s))
        for k, s in reversed(list(enumerate(near)))
    }
    mine = rows_of(core * chips + chip, n_zy), rows_of(chip, n_zy)
    total = sums_all[mine[0], :] + got_core[mine[1], :]
    for k, s in enumerate(near):
        copies[s].wait_recv()
        total = total + got_zy[k].astype(F32)
    sum_zy[...] = total

    copies = [go(sum_zy.at[rows_of(lax.rem(col + d, nx), ROWS)], got_x.at[d - 1], at_x(d)) for d in xs]
    total = sum_zy[rows_of(col, ROWS), :]
    for d in xs:
        copies[d - 1].wait_recv()
        total = total + got_x[d - 1]
    mixed = from_parts(total.astype(BF16).astype(F32), part)
    line[row] = jnp.concatenate([mixed[:, :size], mixed[:, size:]], 0).astype(BF16)

    def spread(ref, done, lag):
        piece = {s: go(ref(row), ref(row), at_zy(s)) for s in near[::-1]}
        pending = [(go(ref(row), ref(row), sibling), chip)]
        done(row)

        def beside():
            copy, source = pending.pop(0)
            copy.wait_recv()
            done(source * CORES + 1 - core)

        for s in near:
            source = chip_at(-s[0], -s[1])
            piece[s].wait_recv()
            came = source * CORES + core
            pending.append((go(ref(came), ref(came), sibling), source))
            done(came)
            if len(pending) > lag:
                beside()
        while pending:
            beside()

    def entries(r):
        both = line[r].astype(F32)
        return jnp.concatenate([both[:ROWS], both[ROWS:]], 1)

    sums = [jnp.zeros((ROWS, press_rows), F32)]

    def product(r):
        of_chip = r // CORES
        at = pl.ds(pl.multiple_of(lax.rem(r, CORES) * width, width), width)
        sums[0] = sums[0] + lax.dot_general(
            entries(r).astype(BF16), bem[of_chip, :, at], NT, preferred_element_type=F32
        )

    for load in loads:
        load.wait()
    spread(lambda r: line.at[r], product, LAG)

    first = row * own
    blocks = chips * CORES
    owner = first // blocks == col
    here = lax.rem(first, blocks)
    same = jnp.concatenate([entries(here + u) for u in range(own)], 1)
    summed = sums[0] + jnp.where(owner, same * self_term[...], 0.0)
    terms[col] = summed[:cases] + summed[cases:]

    copies = [go(terms.at[col], terms.at[col], at_x(d)) for d in xs]
    for copy in copies:
        copy.wait_recv()
    total = terms[0]
    for j in range(1, nx):
        total = total + terms[j]
    rounded = total.astype(BF16)
    press[...] = rounded
    tall = rounded.astype(F32)
    tall = jnp.concatenate([tall, tall], 0)
    tall = jnp.concatenate([tall[:, u * width : (u + 1) * width] for u in range(own)], 0)
    n_own = own * ROWS
    full[rows_of(row, n_own), :] = to_parts(tall.astype(BF16), part).astype(BF16)

    spread(lambda r: full.at[rows_of(r, n_own)], lambda r: None, chips)
    for copy in started:
        copy.wait_send()


def on_device(nx, nz, ny, velocity, pair_struct, pair_panel, pair_count, mortar_coef, bem_matrix, self_term):
    cases = velocity.shape[0]
    slots, panel_size, node_size = mortar_coef.shape
    node_blocks = velocity.shape[1] // (2 * node_size)
    width = 2 * panel_size
    press_rows = bem_matrix.shape[0]
    chips = nz * ny
    col_blocks = chips * CORES
    panel_blocks = nx * col_blocks
    smem = pl.BlockSpec(memory_space=pltpu.SMEM)
    vmem = pl.BlockSpec(memory_space=pltpu.VMEM)
    hbm = pl.BlockSpec(memory_space=pltpu.HBM)
    struct, panel, count = pair_struct[None, :], pair_panel[None, :], pair_count[None, :]

    steps = chips - 1
    sends = 1 + steps + 2 * (nx - 1) + 2 * (2 * steps + 1)
    dma = pltpu.SemaphoreType.DMA
    pressure, full = pl.pallas_call(
        functools.partial(field_kernel, nx, nz, ny),
        out_shape=(
            jax.ShapeDtypeStruct((cases, press_rows), BF16),
            jax.ShapeDtypeStruct((panel_blocks * ROWS, panel_size), BF16),
        ),
        in_specs=[smem] + [hbm] * 6,
        out_specs=(vmem, vmem),
        scratch_shapes=[
            pltpu.SMEM((1, slots), jnp.int32),
            pltpu.SMEM((1, slots), jnp.int32),
            pltpu.VMEM((1, slots), jnp.int32),
            pltpu.VMEM(velocity.shape, BF16),
            pltpu.VMEM(mortar_coef.shape, BF16),
            pltpu.VMEM((chips, press_rows, CORES * width), BF16),
            pltpu.VMEM((1, press_rows), F32),
            pltpu.VMEM((node_blocks, ROWS, 2 * node_size), F32),
            pltpu.VMEM((node_blocks, ROWS, node_size), F32),
            pltpu.VMEM((slots * ROWS, panel_size), F32),
            pltpu.VMEM((panel_blocks * ROWS, panel_size), F32),
            pltpu.VMEM((panel_blocks * ROWS // CORES, panel_size), F32),
            pltpu.VMEM((panel_blocks * ROWS // CORES, panel_size), BF16),
            pltpu.VMEM((steps, nx * ROWS, panel_size), BF16),
            pltpu.VMEM((nx * ROWS, panel_size), F32),
            pltpu.VMEM((nx - 1, ROWS, panel_size), F32),
            pltpu.VMEM((col_blocks, 2 * ROWS, panel_size), BF16),
            pltpu.VMEM((nx, cases, press_rows), F32),
            dma((5,)),
            dma((slots // PER,)),
            dma((chips,)),
            dma((sends,)),
            dma((sends,)),
        ],
        compiler_params=pltpu.CompilerParams(
            collective_id=0, has_side_effects=True, vmem_limit_bytes=44 << 20
        ),
        cost_estimate=pl.CostEstimate(
            flops=2 * cases * bem_matrix.size,
            bytes_accessed=2 * bem_matrix.size,
            transcendentals=0,
        ),
        name="field",
    )(
        count,
        *[
            pltpu.with_memory_space_constraint(x, pltpu.HBM)
            for x in (struct, panel, velocity, mortar_coef, bem_matrix, self_term[None, :])
        ],
    )

    load, pressure = pl.pallas_call(
        backward_kernel,
        out_shape=(
            jax.ShapeDtypeStruct(velocity.shape, F32),
            jax.ShapeDtypeStruct((cases, press_rows), BF16),
        ),
        in_specs=[smem, smem, smem, vmem, vmem, vmem],
        out_specs=(vmem, vmem),
        scratch_shapes=[
            pltpu.VMEM((panel_blocks, ROWS, panel_size), F32),
            pltpu.VMEM((node_blocks, ROWS, node_size), F32),
        ],
        compiler_params=pltpu.CompilerParams(vmem_limit_bytes=24 << 20),
        cost_estimate=pl.CostEstimate(
            flops=2 * ROWS * mortar_coef.size,
            bytes_accessed=2 * mortar_coef.size,
            transcendentals=0,
        ),
        name="mortar_backward",
    )(struct, panel, count, pressure, full, mortar_coef)
    return pressure, load


def solution(mesh):
    nx = mesh.shape["col"]
    chips = mesh.shape["row"] // CORES
    nz = nx if chips % nx == 0 else 1
    placed = (
        P(None, ("col", "row")),
        P(("col", "row")),
        P(("col", "row")),
        P(("col", "row")),
        P(("col", "row"), None, None),
        P("row", "col"),
        P("row"),
    )
    return jax.shard_map(
        functools.partial(on_device, nx, nz, chips // nz),
        mesh=mesh,
        in_specs=placed,
        out_specs=(P(None, "row"), P(None, ("col", "row"))),
        check_vma=False,
    )
```

```python
import functools
import itertools

import jax
import jax.numpy as jnp
from jax import lax
from jax.experimental import pallas as pl
from jax.experimental.pallas import tpu as pltpu
from jax.sharding import PartitionSpec as P

NT = (((1,), (1,)), ((), ()))
NN = (((1,), (0,)), ((), ()))
MESH = pl.DeviceIdType.MESH
F32 = jnp.float32
BF16 = jnp.bfloat16
ROWS = 8
PER = 16
CORES = 2
AHEAD = 3


def parting(width):
    src = lax.broadcasted_iota(jnp.int32, (width, width), 0)
    dst = lax.broadcasted_iota(jnp.int32, (width, width), 1)
    half = width // 2
    to = jnp.where(src % 2 == 1, half, 0) + src // 2
    return jnp.where(to == dst, 1.0, 0.0).astype(BF16)


def first_part(shape):
    return lax.broadcasted_iota(jnp.int32, shape, 0) % ROWS < ROWS // 2


def to_parts(rows, part):
    half = part.shape[0] // 2
    both = lax.dot_general(rows, part, NN, preferred_element_type=F32)
    keep = first_part((rows.shape[0], half))
    return jnp.where(keep, both[:, :half], both[:, half:])


def from_parts(rows, part):
    keep = first_part(rows.shape)
    zero = jnp.zeros_like(rows)
    wide = jnp.concatenate([jnp.where(keep, rows, zero), jnp.where(keep, zero, rows)], 1)
    return lax.dot_general(wide.astype(BF16), part, NT, preferred_element_type=F32)


def pair_term(table, ids, coef, q, dims):
    a, b = table[ids(q)], table[ids(q + 1)]
    zero = jnp.zeros_like(a)
    left = jnp.concatenate(
        [jnp.concatenate([a, zero], 1), jnp.concatenate([zero, b], 1)], 0
    ).astype(BF16)
    right = jnp.concatenate([coef[q], coef[q + 1]], 1 if dims is NT else 0)
    return lax.dot_general(left, right, dims, preferred_element_type=F32)


def backward_kernel(struct, panel, count, press, full, coef, out, press_out, table, acc):
    press_out[...] = press[...]
    table[...] = full[...].astype(F32).reshape(table.shape)
    acc[...] = jnp.zeros_like(acc)
    live = count[0, 0]

    def two(s, carry):
        q = 2 * s
        term = pair_term(table, lambda i: panel[0, i], coef, q, NN)
        for k in range(2):
            where = struct[0, q + k]
            acc[where] = acc[where] + jnp.where(q + k < live, term[k * ROWS : (k + 1) * ROWS], 0.0)
        return carry

    lax.fori_loop(0, coef.shape[0] // 2, two, 0, unroll=min(32, coef.shape[0] // 2))
    blocks, _, half = acc.shape
    part = parting(2 * half)
    rows = acc[...].reshape(blocks * ROWS, half)
    high = rows.astype(BF16).astype(F32)
    mixed = from_parts(high, part) + from_parts(rows - high, part)
    mixed = mixed.reshape(blocks, ROWS, 2 * half)
    cases = out.shape[0]
    for b in range(blocks):
        one = mixed[b]
        out[:, b * 2 * half : (b + 1) * 2 * half] = one[:cases] + one[cases:]


def field_kernel(
    nx, nz, ny, count, struct_any, panel_any, vel_any, coef_any, bem_any, self_any,
    press, full, coef,
    struct, panel, panel_row, vel, bem, self_term, wide, table, pair_rows,
    sums_all, got_core, got_all, line, terms,
    in_sems, coef_sems, bem_sems, send, recv,
):
    col = lax.axis_index("col")
    row = lax.axis_index("row")
    chip, core = row // CORES, row % CORES
    z, y = chip // ny, chip % ny
    chips = nz * ny
    slots, size, _ = coef.shape
    width = 2 * size
    cases, press_rows = press.shape
    own = press_rows // width

    small = [
        (struct_any, struct), (panel_any, panel),
        (panel_any, panel_row), (vel_any, vel), (self_any, self_term),
    ]
    ins = [pltpu.make_async_copy(a, b, in_sems.at[i]) for i, (a, b) in enumerate(small)]
    coefs = [
        pltpu.make_async_copy(
            coef_any.at[pl.ds(i * PER, PER)], coef.at[pl.ds(i * PER, PER)], coef_sems.at[i]
        )
        for i in range(slots // PER)
    ]
    loads = [
        pltpu.make_async_copy(bem_any.at[:, pl.ds(i * width, width)], bem.at[i], bem_sems.at[i])
        for i in range(chips * CORES)
    ]
    for copy in [*ins, *coefs[:AHEAD]]:
        copy.start()

    def chip_at(dz, dy):
        return lax.rem(z + dz + nz, nz) * ny + lax.rem(y + dy + ny, ny)

    def at(step):
        return (lax.rem(col + step[0], nx), row_at(step[1:]))

    def row_at(step):
        return chip_at(*step[:2]) * CORES + (1 - core if step[2] else core)

    def hops(step):
        return sum(min(d, n - d) for d, n in zip(step, (nx, nz, ny)))

    def steps(x_range, cores):
        every = itertools.product(x_range, range(nz), range(ny), range(cores))
        return sorted([s for s in every if any(s)], key=lambda s: (hops(s), s))

    sibling = (0, 0, 0, 1)
    xs = range(1, nx)
    to_owner = steps(range(nx), 1)
    in_col = steps((0,), CORES)
    friends = sorted({*to_owner, *in_col}, key=lambda s: (-hops(s), s))
    barrier = pltpu.get_barrier_semaphore()
    for friend in friends:
        pl.semaphore_signal(barrier, inc=1, device_id=at(friend), device_id_type=MESH)

    started = []

    def go(src, dst, step):
        i = len(started)
        copy = pltpu.make_async_remote_copy(
            src_ref=src, dst_ref=dst, send_sem=send.at[i], recv_sem=recv.at[i],
            device_id=at(step), device_id_type=MESH,
        )
        copy.start()
        started.append(copy)
        return copy

    def rows_of(index, n):
        return pl.ds(pl.multiple_of(index * n, n), n)

    part = parting(width)
    for copy in ins:
        copy.wait()
    vals = vel[...].astype(F32)
    both = jnp.concatenate([vals, vals], 0)
    node_blocks = wide.shape[0]
    for b in range(node_blocks):
        wide[b] = both[:, b * width : (b + 1) * width]
    table[...] = to_parts(
        wide[...].reshape(node_blocks * ROWS, width).astype(BF16), part
    ).reshape(table.shape)
    for i in range(slots // PER):
        coefs[i].wait()
        for copy in coefs[i + AHEAD : i + AHEAD + 1]:
            copy.start()
        if i == len(coefs) - 1:
            for load in loads:
                load.start()

        def two(s, carry, i=i):
            q = i * PER + 2 * s
            term = pair_term(table, lambda j: struct[0, j], coef, q, NT)
            pair_rows[pl.ds(pl.multiple_of(q * ROWS, 2 * ROWS), 2 * ROWS), :] = term
            return carry

        lax.fori_loop(0, PER // 2, two, 0, unroll=PER // 2)

    panel_blocks = nx * chips * CORES
    place = lax.broadcasted_iota(jnp.int32, (panel_blocks, slots), 0)
    block = (place % nx) * (chips * CORES) + (place // nx) % chips * CORES + place // (nx * chips)
    slot = lax.broadcasted_iota(jnp.int32, (panel_blocks, slots), 1)
    hit = (panel_row[...] == block) & (slot < count[0, 0])
    hit = jnp.where(hit, 1.0, 0.0).astype(BF16)
    hit = jnp.concatenate([hit, hit], 1)
    for r in range(ROWS):
        term = pair_rows[pl.ds(r, slots, stride=ROWS), :]
        high = term.astype(BF16)
        low = (term - high.astype(F32)).astype(BF16)
        sums_all[pl.ds(r, panel_blocks, stride=ROWS), :] = lax.dot_general(
            hit, jnp.concatenate([high, low], 0), NN, preferred_element_type=F32
        )

    pl.semaphore_wait(barrier, len(friends))

    n_core = got_core.shape[0]
    copy = go(sums_all.at[rows_of(1 - core, n_core)], got_core, sibling)
    copy.wait_recv()
    got_core[...] = sums_all[rows_of(core, n_core), :] + got_core[...]

    def block_at(step):
        return rows_of(chip_at(*step[1:3]) * nx + lax.rem(col + step[0], nx), ROWS)

    copies = {
        s: go(got_core.at[block_at(s)], got_all.at[k], s)
        for k, s in reversed(list(enumerate(to_owner)))
    }
    total = got_core[block_at((0, 0, 0, 0)), :]
    for k, s in enumerate(to_owner):
        copies[s].wait_recv()
        total = total + got_all[k]
    mixed = from_parts(total.astype(BF16).astype(F32), part)
    line[row] = jnp.concatenate([mixed[:, :size], mixed[:, size:]], 0).astype(BF16)

    def source(s):
        return row_at((-s[1], -s[2], s[3]))

    def send_out(ref, over):
        return {s: go(ref(row), ref(row), s) for s in over[::-1]}

    def came(piece, over):
        over = list(over)
        for s in over:
            piece[s].wait_recv()
        return [source(s) for s in over]

    def entries(r):
        both = line[r].astype(F32)
        return jnp.concatenate([both[:ROWS], both[ROWS:]], 1)

    split = press_rows * 5 // 8

    def products(rows):
        still, moving = 0.0, 0.0
        for r in rows:
            x = entries(r).astype(BF16)
            still += lax.dot_general(x, bem[r, :split], NT, preferred_element_type=F32)
            moving += lax.dot_general(bem[r, split:], x, NT, preferred_element_type=F32)
        return still, moving

    def plus(one, other):
        return one[0] + other[0], one[1] + other[1]

    piece = send_out(lambda r: line.at[r], in_col)
    for load in loads:
        load.wait()
    sums = products([row])
    for _, group in itertools.groupby(in_col, key=hops):
        sums = plus(sums, products(came(piece, group)))
    sums = jnp.concatenate([sums[0], sums[1].T], 1)

    first = row * own
    blocks = chips * CORES
    owner = first // blocks == col
    here = lax.rem(first, blocks)
    same = jnp.concatenate([entries(here + u) for u in range(own)], 1)
    summed = sums + jnp.where(owner, same * self_term[...], 0.0)
    terms[col] = summed[:cases] + summed[cases:]

    copies = [go(terms.at[col], terms.at[col], (d, 0, 0, 0)) for d in xs]
    for copy in copies:
        copy.wait_recv()
    total = terms[0]
    for j in range(1, nx):
        total = total + terms[j]
    rounded = total.astype(BF16)
    press[...] = rounded
    tall = rounded.astype(F32)
    tall = jnp.concatenate([tall, tall], 0)
    tall = jnp.concatenate([tall[:, u * width : (u + 1) * width] for u in range(own)], 0)
    n_own = own * ROWS
    full[rows_of(row, n_own), :] = to_parts(tall.astype(BF16), part).astype(BF16)

    def full_at(r):
        return full.at[rows_of(r, n_own)]

    came(send_out(full_at, in_col), in_col)
    for copy in started:
        copy.wait_send()


def on_device(nx, nz, ny, velocity, pair_struct, pair_panel, pair_count, mortar_coef, bem_matrix, self_term):
    cases = velocity.shape[0]
    slots, panel_size, node_size = mortar_coef.shape
    node_blocks = velocity.shape[1] // (2 * node_size)
    width = 2 * panel_size
    press_rows = bem_matrix.shape[0]
    chips = nz * ny
    col_blocks = chips * CORES
    panel_blocks = nx * col_blocks
    smem = pl.BlockSpec(memory_space=pltpu.SMEM)
    vmem = pl.BlockSpec(memory_space=pltpu.VMEM)
    hbm = pl.BlockSpec(memory_space=pltpu.HBM)
    struct, panel, count = pair_struct[None, :], pair_panel[None, :], pair_count[None, :]

    sends = nx * chips + 2 * (col_blocks - 1) + nx - 1
    dma = pltpu.SemaphoreType.DMA
    pressure, full, coef = pl.pallas_call(
        functools.partial(field_kernel, nx, nz, ny),
        out_shape=(
            jax.ShapeDtypeStruct((cases, press_rows), BF16),
            jax.ShapeDtypeStruct((panel_blocks * ROWS, panel_size), BF16),
            jax.ShapeDtypeStruct(mortar_coef.shape, BF16),
        ),
        in_specs=[smem] + [hbm] * 6,
        out_specs=(vmem, vmem, vmem),
        scratch_shapes=[
            pltpu.SMEM((1, slots), jnp.int32),
            pltpu.SMEM((1, slots), jnp.int32),
            pltpu.VMEM((1, slots), jnp.int32),
            pltpu.VMEM(velocity.shape, BF16),
            pltpu.VMEM((col_blocks, press_rows, width), BF16),
            pltpu.VMEM((1, press_rows), F32),
            pltpu.VMEM((node_blocks, ROWS, 2 * node_size), F32),
            pltpu.VMEM((node_blocks, ROWS, node_size), F32),
            pltpu.VMEM((slots * ROWS, panel_size), F32),
            pltpu.VMEM((panel_blocks * ROWS, panel_size), F32),
            pltpu.VMEM((panel_blocks * ROWS // CORES, panel_size), F32),
            pltpu.VMEM((nx * chips - 1, ROWS, panel_size), F32),
            pltpu.VMEM((col_blocks, 2 * ROWS, panel_size), BF16),
            pltpu.VMEM((nx, cases, press_rows), F32),
            dma((5,)),
            dma((slots // PER,)),
            dma((col_blocks,)),
            dma((sends,)),
            dma((sends,)),
        ],
        compiler_params=pltpu.CompilerParams(
            collective_id=0, has_side_effects=True, vmem_limit_bytes=44 << 20
        ),
        cost_estimate=pl.CostEstimate(
            flops=2 * cases * bem_matrix.size,
            bytes_accessed=2 * bem_matrix.size,
            transcendentals=0,
        ),
        name="field",
    )(
        count,
        *[
            pltpu.with_memory_space_constraint(x, pltpu.HBM)
            for x in (struct, panel, velocity, mortar_coef, bem_matrix, self_term[None, :])
        ],
    )

    load, pressure = pl.pallas_call(
        backward_kernel,
        out_shape=(
            jax.ShapeDtypeStruct(velocity.shape, F32),
            jax.ShapeDtypeStruct((cases, press_rows), BF16),
        ),
        in_specs=[smem, smem, smem, vmem, vmem, vmem],
        out_specs=(vmem, vmem),
        scratch_shapes=[
            pltpu.VMEM((panel_blocks, ROWS, panel_size), F32),
            pltpu.VMEM((node_blocks, ROWS, node_size), F32),
        ],
        compiler_params=pltpu.CompilerParams(vmem_limit_bytes=24 << 20),
        cost_estimate=pl.CostEstimate(
            flops=2 * ROWS * mortar_coef.size,
            bytes_accessed=2 * mortar_coef.size,
            transcendentals=0,
        ),
        name="mortar_backward",
    )(struct, panel, count, pressure, full, coef)
    return pressure, load


def solution(mesh):
    nx = mesh.shape["col"]
    chips = mesh.shape["row"] // CORES
    nz = nx if chips % nx == 0 else 1
    placed = (
        P(None, ("col", "row")),
        P(("col", "row")),
        P(("col", "row")),
        P(("col", "row")),
        P(("col", "row"), None, None),
        P("row", "col"),
        P("row"),
    )
    return jax.shard_map(
        functools.partial(on_device, nx, nz, chips // nz),
        mesh=mesh,
        in_specs=placed,
        out_specs=(P(None, "row"), P(None, ("col", "row"))),
        check_vma=False,
    )
```

```python
import functools
import itertools

import jax
import jax.numpy as jnp
from jax import lax
from jax.experimental import pallas as pl
from jax.experimental.pallas import tpu as pltpu
from jax.sharding import PartitionSpec as P

NT = (((1,), (1,)), ((), ()))
NN = (((1,), (0,)), ((), ()))
MESH = pl.DeviceIdType.MESH
F32 = jnp.float32
BF16 = jnp.bfloat16
ROWS = 8
PER = 32
CORES = 2
AHEAD = 3


def parting(width):
    src = lax.broadcasted_iota(jnp.int32, (width, width), 0)
    dst = lax.broadcasted_iota(jnp.int32, (width, width), 1)
    half = width // 2
    to = jnp.where(src % 2 == 1, half, 0) + src // 2
    return jnp.where(to == dst, 1.0, 0.0).astype(BF16)


def first_part(shape):
    return lax.broadcasted_iota(jnp.int32, shape, 0) % ROWS < ROWS // 2


def to_parts(rows, part):
    half = part.shape[0] // 2
    both = lax.dot_general(rows, part, NN, preferred_element_type=F32)
    keep = first_part((rows.shape[0], half))
    return jnp.where(keep, both[:, :half], both[:, half:])


def from_parts(rows, part):
    keep = first_part(rows.shape)
    zero = jnp.zeros_like(rows)
    wide = jnp.concatenate([jnp.where(keep, rows, zero), jnp.where(keep, zero, rows)], 1)
    return lax.dot_general(wide.astype(BF16), part, NT, preferred_element_type=F32)


def pair_term(table, ids, coef, q, dims):
    a, b = table[ids(q)], table[ids(q + 1)]
    zero = jnp.zeros_like(a)
    left = jnp.concatenate(
        [jnp.concatenate([a, zero], 1), jnp.concatenate([zero, b], 1)], 0
    ).astype(BF16)
    right = jnp.concatenate([coef[q], coef[q + 1]], 1 if dims is NT else 0)
    return lax.dot_general(left, right, dims, preferred_element_type=F32)


def backward_kernel(struct, panel, count, press, full, coef, out, press_out, table, acc):
    press_out[...] = press[...]
    table[...] = full[...].astype(F32).reshape(table.shape)
    acc[...] = jnp.zeros_like(acc)
    live = count[0, 0]

    def two(s, carry):
        q = 2 * s
        term = pair_term(table, lambda i: panel[0, i], coef, q, NN)
        for k in range(2):
            where = struct[0, q + k]
            acc[where] = acc[where] + jnp.where(q + k < live, term[k * ROWS : (k + 1) * ROWS], 0.0)
        return carry

    lax.fori_loop(0, coef.shape[0] // 2, two, 0, unroll=min(32, coef.shape[0] // 2))
    blocks, _, half = acc.shape
    part = parting(2 * half)
    rows = acc[...].reshape(blocks * ROWS, half)
    high = rows.astype(BF16).astype(F32)
    mixed = from_parts(high, part) + from_parts(rows - high, part)
    mixed = mixed.reshape(blocks, ROWS, 2 * half)
    cases = out.shape[0]
    for b in range(blocks):
        one = mixed[b]
        out[:, b * 2 * half : (b + 1) * 2 * half] = one[:cases] + one[cases:]


def field_kernel(
    nx, nz, ny, count, struct_any, panel_any, vel_any, coef_any, bem_any, self_any,
    press, full, coef,
    struct, panel, panel_row, vel, bem, self_term, wide, table, pair_rows,
    other_half, own_half, got_core, got_all, line, terms,
    in_sems, coef_sems, bem_sems, send, recv,
):
    col = lax.axis_index("col")
    row = lax.axis_index("row")
    chip, core = row // CORES, row % CORES
    z, y = chip // ny, chip % ny
    chips = nz * ny
    slots, size, _ = coef.shape
    width = 2 * size
    cases, press_rows = press.shape
    own = press_rows // width

    small = [
        (struct_any, struct), (panel_any, panel),
        (panel_any, panel_row), (vel_any, vel), (self_any, self_term),
    ]
    ins = [pltpu.make_async_copy(a, b, in_sems.at[i]) for i, (a, b) in enumerate(small)]
    coefs = [
        pltpu.make_async_copy(
            coef_any.at[pl.ds(i * PER, PER)], coef.at[pl.ds(i * PER, PER)], coef_sems.at[i]
        )
        for i in range(slots // PER)
    ]
    loads = [
        pltpu.make_async_copy(bem_any.at[:, pl.ds(i * width, width)], bem.at[i], bem_sems.at[i])
        for i in range(chips * CORES)
    ]
    for copy in [*ins, *coefs[:AHEAD]]:
        copy.start()

    def chip_at(dz, dy):
        return lax.rem(z + dz + nz, nz) * ny + lax.rem(y + dy + ny, ny)

    def at(step):
        return (lax.rem(col + step[0], nx), row_at(step[1:]))

    def row_at(step):
        return chip_at(*step[:2]) * CORES + (1 - core if step[2] else core)

    def hops(step):
        return sum(min(d, n - d) for d, n in zip(step, (nx, nz, ny)))

    def steps(x_range, cores):
        every = itertools.product(x_range, range(nz), range(ny), range(cores))
        return sorted([s for s in every if any(s)], key=lambda s: (hops(s), s))

    sibling = (0, 0, 0, 1)
    xs = range(1, nx)
    to_owner = steps(range(nx), 1)
    in_col = steps((0,), CORES)
    friends = [*to_owner[::-1], sibling]
    barrier = pltpu.get_barrier_semaphore()
    for friend in friends:
        pl.semaphore_signal(barrier, inc=1, device_id=at(friend), device_id_type=MESH)

    started = []

    def go(src, dst, step):
        i = len(started)
        copy = pltpu.make_async_remote_copy(
            src_ref=src, dst_ref=dst, send_sem=send.at[i], recv_sem=recv.at[i],
            device_id=at(step), device_id_type=MESH,
        )
        copy.start()
        started.append(copy)
        return copy

    def rows_of(index, n):
        return pl.ds(pl.multiple_of(index * n, n), n)

    part = parting(width)
    for copy in ins:
        copy.wait()
    vals = vel[...].astype(F32)
    both = jnp.concatenate([vals, vals], 0)
    node_blocks = wide.shape[0]
    for b in range(node_blocks):
        wide[b] = both[:, b * width : (b + 1) * width]
    table[...] = to_parts(
        wide[...].reshape(node_blocks * ROWS, width).astype(BF16), part
    ).reshape(table.shape)
    for i in range(slots // PER):
        coefs[i].wait()
        for copy in coefs[i + AHEAD : i + AHEAD + 1]:
            copy.start()
        if i == len(coefs) - 1:
            for load in loads:
                load.start()

        def two(s, carry, i=i):
            q = i * PER + 2 * s
            term = pair_term(table, lambda j: struct[0, j], coef, q, NT)
            pair_rows[pl.ds(pl.multiple_of(q * ROWS, 2 * ROWS), 2 * ROWS), :] = term
            return carry

        lax.fori_loop(0, PER // 2, two, 0, unroll=PER // 2)

    terms_16 = []
    for r in range(ROWS):
        term = pair_rows[pl.ds(r, slots, stride=ROWS), :]
        high = term.astype(BF16)
        low = (term - high.astype(F32)).astype(BF16)
        terms_16.append(jnp.concatenate([high, low], 0))
    half_blocks = nx * chips
    place = lax.broadcasted_iota(jnp.int32, (half_blocks, slots), 0)
    block = (place % nx) * (chips * CORES) + place // nx * CORES
    slot = lax.broadcasted_iota(jnp.int32, (half_blocks, slots), 1)
    live = slot < count[0, 0]

    def block_sums(of_core, into):
        hit = jnp.where((panel_row[...] == block + of_core) & live, 1.0, 0.0).astype(BF16)
        hit = jnp.concatenate([hit, hit], 1)
        for r in range(ROWS):
            into[pl.ds(r, half_blocks, stride=ROWS), :] = lax.dot_general(
                hit, terms_16[r], NN, preferred_element_type=F32
            )

    block_sums(1 - core, other_half)
    pl.semaphore_wait(barrier, len(friends))
    copy = go(other_half, got_core, sibling)
    block_sums(core, own_half)
    copy.wait_recv()
    got_core[...] = own_half[...] + got_core[...]

    def block_at(step):
        return rows_of(chip_at(*step[1:3]) * nx + lax.rem(col + step[0], nx), ROWS)

    copies = {
        s: go(got_core.at[block_at(s)], got_all.at[k], s)
        for k, s in reversed(list(enumerate(to_owner)))
    }
    total = got_core[block_at((0, 0, 0, 0)), :]
    for k, s in enumerate(to_owner):
        copies[s].wait_recv()
        total = total + got_all[k]
    mixed = from_parts(total.astype(BF16).astype(F32), part)
    line[row] = jnp.concatenate([mixed[:, :size], mixed[:, size:]], 0).astype(BF16)

    def source(s):
        return row_at((-s[1], -s[2], s[3]))

    def send_out(ref, over):
        return {s: go(ref(row), ref(row), s) for s in over[::-1]}

    def came(piece, over):
        over = list(over)
        for s in over:
            piece[s].wait_recv()
        return [source(s) for s in over]

    def entries(r):
        both = line[r].astype(F32)
        return jnp.concatenate([both[:ROWS], both[ROWS:]], 1)

    split = press_rows * 5 // 8

    def products(rows):
        still, moving = 0.0, 0.0
        for r in rows:
            x = entries(r).astype(BF16)
            still += lax.dot_general(x, bem[r, :split], NT, preferred_element_type=F32)
            moving += lax.dot_general(bem[r, split:], x, NT, preferred_element_type=F32)
        return still, moving

    def plus(one, other):
        return one[0] + other[0], one[1] + other[1]

    piece = send_out(lambda r: line.at[r], in_col)
    for load in loads:
        load.wait()
    sums = products([row])
    for _, group in itertools.groupby(in_col, key=hops):
        sums = plus(sums, products(came(piece, group)))
    sums = jnp.concatenate([sums[0], sums[1].T], 1)

    first = row * own
    blocks = chips * CORES
    owner = first // blocks == col
    here = lax.rem(first, blocks)
    same = jnp.concatenate([entries(here + u) for u in range(own)], 1)
    summed = sums + jnp.where(owner, same * self_term[...], 0.0)
    terms[col] = summed[:cases] + summed[cases:]

    copies = [go(terms.at[col], terms.at[col], (d, 0, 0, 0)) for d in xs]
    for copy in copies:
        copy.wait_recv()
    total = terms[0]
    for j in range(1, nx):
        total = total + terms[j]
    rounded = total.astype(BF16)
    press[...] = rounded
    tall = rounded.astype(F32)
    tall = jnp.concatenate([tall, tall], 0)
    tall = jnp.concatenate([tall[:, u * width : (u + 1) * width] for u in range(own)], 0)
    n_own = own * ROWS
    full[rows_of(row, n_own), :] = to_parts(tall.astype(BF16), part).astype(BF16)

    def full_at(r):
        return full.at[rows_of(r, n_own)]

    came(send_out(full_at, in_col), in_col)
    for copy in started:
        copy.wait_send()


def on_device(nx, nz, ny, velocity, pair_struct, pair_panel, pair_count, mortar_coef, bem_matrix, self_term):
    cases = velocity.shape[0]
    slots, panel_size, node_size = mortar_coef.shape
    node_blocks = velocity.shape[1] // (2 * node_size)
    width = 2 * panel_size
    press_rows = bem_matrix.shape[0]
    chips = nz * ny
    col_blocks = chips * CORES
    panel_blocks = nx * col_blocks
    smem = pl.BlockSpec(memory_space=pltpu.SMEM)
    vmem = pl.BlockSpec(memory_space=pltpu.VMEM)
    hbm = pl.BlockSpec(memory_space=pltpu.HBM)
    struct, panel, count = pair_struct[None, :], pair_panel[None, :], pair_count[None, :]

    sends = nx * chips + 2 * (col_blocks - 1) + nx - 1
    dma = pltpu.SemaphoreType.DMA
    pressure, full, coef = pl.pallas_call(
        functools.partial(field_kernel, nx, nz, ny),
        out_shape=(
            jax.ShapeDtypeStruct((cases, press_rows), BF16),
            jax.ShapeDtypeStruct((panel_blocks * ROWS, panel_size), BF16),
            jax.ShapeDtypeStruct(mortar_coef.shape, BF16),
        ),
        in_specs=[smem] + [hbm] * 6,
        out_specs=(vmem, vmem, vmem),
        scratch_shapes=[
            pltpu.SMEM((1, slots), jnp.int32),
            pltpu.SMEM((1, slots), jnp.int32),
            pltpu.VMEM((1, slots), jnp.int32),
            pltpu.VMEM(velocity.shape, BF16),
            pltpu.VMEM((col_blocks, press_rows, width), BF16),
            pltpu.VMEM((1, press_rows), F32),
            pltpu.VMEM((node_blocks, ROWS, 2 * node_size), F32),
            pltpu.VMEM((node_blocks, ROWS, node_size), F32),
            pltpu.VMEM((slots * ROWS, panel_size), F32),
            pltpu.VMEM((panel_blocks * ROWS // CORES, panel_size), F32),
            pltpu.VMEM((panel_blocks * ROWS // CORES, panel_size), F32),
            pltpu.VMEM((panel_blocks * ROWS // CORES, panel_size), F32),
            pltpu.VMEM((nx * chips - 1, ROWS, panel_size), F32),
            pltpu.VMEM((col_blocks, 2 * ROWS, panel_size), BF16),
            pltpu.VMEM((nx, cases, press_rows), F32),
            dma((5,)),
            dma((slots // PER,)),
            dma((col_blocks,)),
            dma((sends,)),
            dma((sends,)),
        ],
        compiler_params=pltpu.CompilerParams(
            collective_id=0, has_side_effects=True, vmem_limit_bytes=44 << 20
        ),
        cost_estimate=pl.CostEstimate(
            flops=2 * cases * bem_matrix.size,
            bytes_accessed=2 * bem_matrix.size,
            transcendentals=0,
        ),
        name="field",
    )(
        count,
        *[
            pltpu.with_memory_space_constraint(x, pltpu.HBM)
            for x in (struct, panel, velocity, mortar_coef, bem_matrix, self_term[None, :])
        ],
    )

    load, pressure = pl.pallas_call(
        backward_kernel,
        out_shape=(
            jax.ShapeDtypeStruct(velocity.shape, F32),
            jax.ShapeDtypeStruct((cases, press_rows), BF16),
        ),
        in_specs=[smem, smem, smem, vmem, vmem, vmem],
        out_specs=(vmem, vmem),
        scratch_shapes=[
            pltpu.VMEM((panel_blocks, ROWS, panel_size), F32),
            pltpu.VMEM((node_blocks, ROWS, node_size), F32),
        ],
        compiler_params=pltpu.CompilerParams(vmem_limit_bytes=24 << 20),
        cost_estimate=pl.CostEstimate(
            flops=2 * ROWS * mortar_coef.size,
            bytes_accessed=2 * mortar_coef.size,
            transcendentals=0,
        ),
        name="mortar_backward",
    )(struct, panel, count, pressure, full, coef)
    return pressure, load


def solution(mesh):
    nx = mesh.shape["col"]
    chips = mesh.shape["row"] // CORES
    nz = nx if chips % nx == 0 else 1
    placed = (
        P(None, ("col", "row")),
        P(("col", "row")),
        P(("col", "row")),
        P(("col", "row")),
        P(("col", "row"), None, None),
        P("row", "col"),
        P("row"),
    )
    return jax.shard_map(
        functools.partial(on_device, nx, nz, chips // nz),
        mesh=mesh,
        in_specs=placed,
        out_specs=(P(None, "row"), P(None, ("col", "row"))),
        check_vma=False,
    )
```

```python
import functools
import itertools

import jax
import jax.numpy as jnp
from jax import lax
from jax.experimental import pallas as pl
from jax.experimental.pallas import tpu as pltpu
from jax.sharding import PartitionSpec as P

NT = (((1,), (1,)), ((), ()))
NN = (((1,), (0,)), ((), ()))
MESH = pl.DeviceIdType.MESH
F32 = jnp.float32
BF16 = jnp.bfloat16
ROWS = 8
PER = 64
CORES = 2
AHEAD = 8


def parting(width):
    src = lax.broadcasted_iota(jnp.int32, (width, width), 0)
    dst = lax.broadcasted_iota(jnp.int32, (width, width), 1)
    half = width // 2
    to = jnp.where(src % 2 == 1, half, 0) + src // 2
    return jnp.where(to == dst, 1.0, 0.0).astype(BF16)


def first_part(shape):
    return lax.broadcasted_iota(jnp.int32, shape, 0) % ROWS < ROWS // 2


def to_parts(rows, part):
    half = part.shape[0] // 2
    both = lax.dot_general(rows, part, NN, preferred_element_type=F32)
    keep = first_part((rows.shape[0], half))
    return jnp.where(keep, both[:, :half], both[:, half:])


def from_parts(rows, part):
    keep = first_part(rows.shape)
    zero = jnp.zeros_like(rows)
    wide = jnp.concatenate([jnp.where(keep, rows, zero), jnp.where(keep, zero, rows)], 1)
    return lax.dot_general(wide.astype(BF16), part, NT, preferred_element_type=F32)


def pair_term(table, ids, coef, q, dims):
    a, b = table[ids(q)], table[ids(q + 1)]
    zero = jnp.zeros_like(a)
    left = jnp.concatenate(
        [jnp.concatenate([a, zero], 1), jnp.concatenate([zero, b], 1)], 0
    ).astype(BF16)
    right = jnp.concatenate([coef[q], coef[q + 1]], 1 if dims is NT else 0)
    return lax.dot_general(left, right, dims, preferred_element_type=F32)


def backward_kernel(struct, panel, count, press, full, coef, out, press_out, table, acc):
    press_out[...] = press[...]
    table[...] = full[...].astype(F32).reshape(table.shape)
    acc[...] = jnp.zeros_like(acc)
    live = count[0, 0]

    def two(s, carry):
        q = 2 * s
        term = pair_term(table, lambda i: panel[0, i], coef, q, NN)
        for k in range(2):
            where = struct[0, q + k]
            acc[where] = acc[where] + jnp.where(q + k < live, term[k * ROWS : (k + 1) * ROWS], 0.0)
        return carry

    lax.fori_loop(0, coef.shape[0] // 2, two, 0, unroll=coef.shape[0] // 2)
    blocks, _, half = acc.shape
    part = parting(2 * half)
    rows = acc[...].reshape(blocks * ROWS, half)
    high = rows.astype(BF16).astype(F32)
    mixed = from_parts(high, part) + from_parts(rows - high, part)
    mixed = mixed.reshape(blocks, ROWS, 2 * half)
    cases = out.shape[0]
    for b in range(blocks):
        one = mixed[b]
        out[:, b * 2 * half : (b + 1) * 2 * half] = one[:cases] + one[cases:]


def field_kernel(
    nx, nz, ny, count, struct_any, panel_any, vel_any, coef_any, bem_any, self_any,
    press, full, coef,
    struct, panel, panel_row, vel, bem, self_term, wide, table, pair_rows,
    other_half, own_half, got_core, got_all, line, terms,
    in_sems, coef_sems, bem_sems, send, recv,
):
    col = lax.axis_index("col")
    row = lax.axis_index("row")
    chip, core = row // CORES, row % CORES
    z, y = chip // ny, chip % ny
    chips = nz * ny
    slots, size, _ = coef.shape
    width = 2 * size
    cases, press_rows = press.shape
    own = press_rows // width

    small = [
        (struct_any, struct), (panel_any, panel),
        (panel_any, panel_row), (vel_any, vel), (self_any, self_term),
    ]
    ins = [pltpu.make_async_copy(a, b, in_sems.at[i]) for i, (a, b) in enumerate(small)]
    coefs = [
        pltpu.make_async_copy(
            coef_any.at[pl.ds(i * PER, PER)], coef.at[pl.ds(i * PER, PER)], coef_sems.at[i]
        )
        for i in range(slots // PER)
    ]
    loads = [
        pltpu.make_async_copy(bem_any.at[:, pl.ds(i * width, width)], bem.at[i], bem_sems.at[i])
        for i in range(chips * CORES)
    ]
    for copy in [*ins, *coefs[:AHEAD]]:
        copy.start()

    def chip_at(dz, dy):
        return lax.rem(z + dz + nz, nz) * ny + lax.rem(y + dy + ny, ny)

    def at(step):
        return (lax.rem(col + step[0], nx), row_at(step[1:]))

    def row_at(step):
        return chip_at(*step[:2]) * CORES + (1 - core if step[2] else core)

    def hops(step):
        return sum(min(d, n - d) for d, n in zip(step, (nx, nz, ny)))

    def steps(x_range, cores):
        every = itertools.product(x_range, range(nz), range(ny), range(cores))
        return sorted([s for s in every if any(s)], key=lambda s: (hops(s), s))

    sibling = (0, 0, 0, 1)
    xs = range(1, nx)
    to_owner = steps(range(nx), 1)
    in_col = steps((0,), CORES)
    friends = [*to_owner[::-1], sibling]
    barrier = pltpu.get_barrier_semaphore()
    for friend in friends:
        pl.semaphore_signal(barrier, inc=1, device_id=at(friend), device_id_type=MESH)

    started = []

    def go(src, dst, step):
        i = len(started)
        copy = pltpu.make_async_remote_copy(
            src_ref=src, dst_ref=dst, send_sem=send.at[i], recv_sem=recv.at[i],
            device_id=at(step), device_id_type=MESH,
        )
        copy.start()
        started.append(copy)
        return copy

    def rows_of(index, n):
        return pl.ds(pl.multiple_of(index * n, n), n)

    part = parting(width)
    for copy in ins:
        copy.wait()
    vals = vel[...].astype(F32)
    both = jnp.concatenate([vals, vals], 0)
    node_blocks = wide.shape[0]
    for b in range(node_blocks):
        wide[b] = both[:, b * width : (b + 1) * width]
    table[...] = to_parts(
        wide[...].reshape(node_blocks * ROWS, width).astype(BF16), part
    ).reshape(table.shape)
    for i in range(slots // PER):
        coefs[i].wait()
        for copy in coefs[i + AHEAD : i + AHEAD + 1]:
            copy.start()
        if i == len(coefs) - 1:
            for load in loads:
                load.start()

        def two(s, carry, i=i):
            q = i * PER + 2 * s
            term = pair_term(table, lambda j: struct[0, j], coef, q, NT)
            pair_rows[pl.ds(pl.multiple_of(q * ROWS, 2 * ROWS), 2 * ROWS), :] = term
            return carry

        lax.fori_loop(0, PER // 2, two, 0, unroll=PER // 2)

    terms_16 = []
    for r in range(ROWS):
        term = pair_rows[pl.ds(r, slots, stride=ROWS), :]
        high = term.astype(BF16)
        low = (term - high.astype(F32)).astype(BF16)
        terms_16.append(jnp.concatenate([high, low], 0))
    half_blocks = nx * chips
    place = lax.broadcasted_iota(jnp.int32, (half_blocks, slots), 0)
    block = (place % nx) * (chips * CORES) + place // nx * CORES
    slot = lax.broadcasted_iota(jnp.int32, (half_blocks, slots), 1)
    live = slot < count[0, 0]

    def block_sums(of_core, into):
        hit = jnp.where((panel_row[...] == block + of_core) & live, 1.0, 0.0).astype(BF16)
        hit = jnp.concatenate([hit, hit], 1)
        for r in range(ROWS):
            into[pl.ds(r, half_blocks, stride=ROWS), :] = lax.dot_general(
                hit, terms_16[r], NN, preferred_element_type=F32
            )

    block_sums(1 - core, other_half)
    pl.semaphore_wait(barrier, len(friends))
    copy = go(other_half, got_core, sibling)
    block_sums(core, own_half)
    copy.wait_recv()
    got_core[...] = own_half[...] + got_core[...]

    def block_at(step):
        return rows_of(chip_at(*step[1:3]) * nx + lax.rem(col + step[0], nx), ROWS)

    copies = {
        s: go(got_core.at[block_at(s)], got_all.at[k], s)
        for k, s in reversed(list(enumerate(to_owner)))
    }
    total = got_core[block_at((0, 0, 0, 0)), :]
    for k, s in enumerate(to_owner):
        copies[s].wait_recv()
        total = total + got_all[k]
    mixed = from_parts(total.astype(BF16).astype(F32), part)
    line[row] = jnp.concatenate([mixed[:, :size], mixed[:, size:]], 0).astype(BF16)

    def source(s):
        return row_at((-s[1], -s[2], s[3]))

    def send_out(ref, over):
        return {s: go(ref(row), ref(row), s) for s in over[::-1]}

    def came(piece, over):
        over = list(over)
        for s in over:
            piece[s].wait_recv()
        return [source(s) for s in over]

    def entries(r):
        both = line[r].astype(F32)
        return jnp.concatenate([both[:ROWS], both[ROWS:]], 1)

    split = press_rows * 5 // 8

    def products(rows):
        still, moving = 0.0, 0.0
        for r in rows:
            x = entries(r).astype(BF16)
            still += lax.dot_general(x, bem[r, :split], NT, preferred_element_type=F32)
            moving += lax.dot_general(bem[r, split:], x, NT, preferred_element_type=F32)
        return still, moving

    def plus(one, other):
        return one[0] + other[0], one[1] + other[1]

    piece = send_out(lambda r: line.at[r], in_col)
    for load in loads:
        load.wait()
    sums = products([row])
    for _, group in itertools.groupby(in_col, key=hops):
        sums = plus(sums, products(came(piece, group)))
    sums = jnp.concatenate([sums[0], sums[1].T], 1)

    first = row * own
    blocks = chips * CORES
    owner = first // blocks == col
    here = lax.rem(first, blocks)
    same = jnp.concatenate([entries(here + u) for u in range(own)], 1)
    summed = sums + jnp.where(owner, same * self_term[...], 0.0)
    terms[col] = summed[:cases] + summed[cases:]

    copies = [go(terms.at[col], terms.at[col], (d, 0, 0, 0)) for d in xs]
    for copy in copies:
        copy.wait_recv()
    total = terms[0]
    for j in range(1, nx):
        total = total + terms[j]
    rounded = total.astype(BF16)
    press[...] = rounded
    tall = rounded.astype(F32)
    tall = jnp.concatenate([tall, tall], 0)
    tall = jnp.concatenate([tall[:, u * width : (u + 1) * width] for u in range(own)], 0)
    n_own = own * ROWS
    full[rows_of(row, n_own), :] = to_parts(tall.astype(BF16), part).astype(BF16)

    def full_at(r):
        return full.at[rows_of(r, n_own)]

    came(send_out(full_at, in_col), in_col)
    for copy in started:
        copy.wait_send()


def on_device(nx, nz, ny, velocity, pair_struct, pair_panel, pair_count, mortar_coef, bem_matrix, self_term):
    cases = velocity.shape[0]
    slots, panel_size, node_size = mortar_coef.shape
    node_blocks = velocity.shape[1] // (2 * node_size)
    width = 2 * panel_size
    press_rows = bem_matrix.shape[0]
    chips = nz * ny
    col_blocks = chips * CORES
    panel_blocks = nx * col_blocks
    smem = pl.BlockSpec(memory_space=pltpu.SMEM)
    vmem = pl.BlockSpec(memory_space=pltpu.VMEM)
    hbm = pl.BlockSpec(memory_space=pltpu.HBM)
    struct, panel, count = pair_struct[None, :], pair_panel[None, :], pair_count[None, :]

    sends = nx * chips + 2 * (col_blocks - 1) + nx - 1
    dma = pltpu.SemaphoreType.DMA
    pressure, full, coef = pl.pallas_call(
        functools.partial(field_kernel, nx, nz, ny),
        out_shape=(
            jax.ShapeDtypeStruct((cases, press_rows), BF16),
            jax.ShapeDtypeStruct((panel_blocks * ROWS, panel_size), BF16),
            jax.ShapeDtypeStruct(mortar_coef.shape, BF16),
        ),
        in_specs=[smem] + [hbm] * 6,
        out_specs=(vmem, vmem, vmem),
        scratch_shapes=[
            pltpu.SMEM((1, slots), jnp.int32),
            pltpu.SMEM((1, slots), jnp.int32),
            pltpu.VMEM((1, slots), jnp.int32),
            pltpu.VMEM(velocity.shape, BF16),
            pltpu.VMEM((col_blocks, press_rows, width), BF16),
            pltpu.VMEM((1, press_rows), F32),
            pltpu.VMEM((node_blocks, ROWS, 2 * node_size), F32),
            pltpu.VMEM((node_blocks, ROWS, node_size), F32),
            pltpu.VMEM((slots * ROWS, panel_size), F32),
            pltpu.VMEM((panel_blocks * ROWS // CORES, panel_size), F32),
            pltpu.VMEM((panel_blocks * ROWS // CORES, panel_size), F32),
            pltpu.VMEM((panel_blocks * ROWS // CORES, panel_size), F32),
            pltpu.VMEM((nx * chips - 1, ROWS, panel_size), F32),
            pltpu.VMEM((col_blocks, 2 * ROWS, panel_size), BF16),
            pltpu.VMEM((nx, cases, press_rows), F32),
            dma((5,)),
            dma((slots // PER,)),
            dma((col_blocks,)),
            dma((sends,)),
            dma((sends,)),
        ],
        compiler_params=pltpu.CompilerParams(
            collective_id=0, has_side_effects=True, vmem_limit_bytes=44 << 20
        ),
        cost_estimate=pl.CostEstimate(
            flops=2 * cases * bem_matrix.size,
            bytes_accessed=2 * bem_matrix.size,
            transcendentals=0,
        ),
        name="field",
    )(
        count,
        *[
            pltpu.with_memory_space_constraint(x, pltpu.HBM)
            for x in (struct, panel, velocity, mortar_coef, bem_matrix, self_term[None, :])
        ],
    )

    load, pressure = pl.pallas_call(
        backward_kernel,
        out_shape=(
            jax.ShapeDtypeStruct(velocity.shape, F32),
            jax.ShapeDtypeStruct((cases, press_rows), BF16),
        ),
        in_specs=[smem, smem, smem, vmem, vmem, vmem],
        out_specs=(vmem, vmem),
        scratch_shapes=[
            pltpu.VMEM((panel_blocks, ROWS, panel_size), F32),
            pltpu.VMEM((node_blocks, ROWS, node_size), F32),
        ],
        compiler_params=pltpu.CompilerParams(vmem_limit_bytes=24 << 20),
        cost_estimate=pl.CostEstimate(
            flops=2 * ROWS * mortar_coef.size,
            bytes_accessed=2 * mortar_coef.size,
            transcendentals=0,
        ),
        name="mortar_backward",
    )(struct, panel, count, pressure, full, coef)
    return pressure, load


def solution(mesh):
    nx = mesh.shape["col"]
    chips = mesh.shape["row"] // CORES
    nz = nx if chips % nx == 0 else 1
    placed = (
        P(None, ("col", "row")),
        P(("col", "row")),
        P(("col", "row")),
        P(("col", "row")),
        P(("col", "row"), None, None),
        P("row", "col"),
        P("row"),
    )
    return jax.shard_map(
        functools.partial(on_device, nx, nz, chips // nz),
        mesh=mesh,
        in_specs=placed,
        out_specs=(P(None, "row"), P(None, ("col", "row"))),
        check_vma=False,
    )
```

```python
import functools
import itertools

import jax
import jax.numpy as jnp
from jax import lax
from jax.experimental import pallas as pl
from jax.experimental.pallas import tpu as pltpu
from jax.sharding import PartitionSpec as P

NT = (((1,), (1,)), ((), ()))
NN = (((1,), (0,)), ((), ()))
MESH = pl.DeviceIdType.MESH
F32 = jnp.float32
BF16 = jnp.bfloat16
ROWS = 8
PER = 64
CORES = 2
AHEAD = 8


def parting(width):
    src = lax.broadcasted_iota(jnp.int32, (width, width), 0)
    dst = lax.broadcasted_iota(jnp.int32, (width, width), 1)
    half = width // 2
    to = jnp.where(src % 2 == 1, half, 0) + src // 2
    return jnp.where(to == dst, 1.0, 0.0).astype(BF16)


def first_part(shape):
    return lax.broadcasted_iota(jnp.int32, shape, 0) % ROWS < ROWS // 2


def to_parts(rows, part):
    half = part.shape[0] // 2
    both = lax.dot_general(rows, part, NN, preferred_element_type=F32)
    keep = first_part((rows.shape[0], half))
    return jnp.where(keep, both[:, :half], both[:, half:])


def from_parts(rows, part):
    keep = first_part(rows.shape)
    zero = jnp.zeros_like(rows)
    wide = jnp.concatenate([jnp.where(keep, rows, zero), jnp.where(keep, zero, rows)], 1)
    return lax.dot_general(wide.astype(BF16), part, NT, preferred_element_type=F32)


def pair_term(table, ids, coef, q, dims):
    a, b = table[ids(q)], table[ids(q + 1)]
    zero = jnp.zeros_like(a)
    left = jnp.concatenate(
        [jnp.concatenate([a, zero], 1), jnp.concatenate([zero, b], 1)], 0
    ).astype(BF16)
    right = jnp.concatenate([coef[q], coef[q + 1]], 1 if dims is NT else 0)
    return lax.dot_general(left, right, dims, preferred_element_type=F32)


def backward_kernel(struct, panel, count, press, full, coef, out, press_out, table, acc):
    press_out[...] = press[...]
    table[...] = full[...].astype(F32).reshape(table.shape)
    acc[...] = jnp.zeros_like(acc)
    live = count[0, 0]

    def two(s, carry):
        q = 2 * s
        term = pair_term(table, lambda i: panel[0, i], coef, q, NN)
        for k in range(2):
            where = struct[0, q + k]
            acc[where] = acc[where] + jnp.where(q + k < live, term[k * ROWS : (k + 1) * ROWS], 0.0)
        return carry

    lax.fori_loop(0, coef.shape[0] // 2, two, 0, unroll=coef.shape[0] // 2)
    blocks, _, half = acc.shape
    part = parting(2 * half)
    rows = acc[...].reshape(blocks * ROWS, half)
    high = rows.astype(BF16).astype(F32)
    mixed = from_parts(high, part) + from_parts(rows - high, part)
    mixed = mixed.reshape(blocks, ROWS, 2 * half)
    cases = out.shape[0]
    for b in range(blocks):
        one = mixed[b]
        out[:, b * 2 * half : (b + 1) * 2 * half] = one[:cases] + one[cases:]


def field_kernel(
    nx, nz, ny, count, struct_any, panel_any, vel_any, coef_any, bem_any, self_any,
    press, full, coef,
    struct, panel, panel_row, vel, bem, self_term, wide, table, pair_rows,
    other_half, own_half, got_core, got_all, line, terms,
    in_sems, coef_sems, bem_sems, send, recv,
):
    col = lax.axis_index("col")
    row = lax.axis_index("row")
    chip, core = row // CORES, row % CORES
    z, y = chip // ny, chip % ny
    chips = nz * ny
    slots, size, _ = coef.shape
    width = 2 * size
    cases, press_rows = press.shape
    own = press_rows // width

    small = [
        (struct_any, struct), (panel_any, panel),
        (panel_any, panel_row), (vel_any, vel), (self_any, self_term),
    ]
    ins = [pltpu.make_async_copy(a, b, in_sems.at[i]) for i, (a, b) in enumerate(small)]
    coefs = [
        pltpu.make_async_copy(
            coef_any.at[pl.ds(i * PER, PER)], coef.at[pl.ds(i * PER, PER)], coef_sems.at[i]
        )
        for i in range(slots // PER)
    ]
    loads = [
        pltpu.make_async_copy(bem_any.at[:, pl.ds(i * width, width)], bem.at[i], bem_sems.at[i])
        for i in range(chips * CORES)
    ]
    for copy in [*ins, *coefs[:AHEAD]]:
        copy.start()

    def chip_at(dz, dy):
        return lax.rem(z + dz + nz, nz) * ny + lax.rem(y + dy + ny, ny)

    def at(step):
        return (lax.rem(col + step[0], nx), row_at(step[1:]))

    def row_at(step):
        return chip_at(*step[:2]) * CORES + (1 - core if step[2] else core)

    def hops(step):
        return sum(min(d, n - d) for d, n in zip(step, (nx, nz, ny)))

    def steps(x_range, cores):
        every = itertools.product(x_range, range(nz), range(ny), range(cores))
        return sorted([s for s in every if any(s)], key=lambda s: (hops(s), s))

    sibling = (0, 0, 0, 1)
    xs = range(1, nx)
    to_owner = steps(range(nx), 1)
    in_col = steps((0,), CORES)
    friends = [*to_owner[::-1], sibling]
    barrier = pltpu.get_barrier_semaphore()
    for friend in friends:
        pl.semaphore_signal(barrier, inc=1, device_id=at(friend), device_id_type=MESH)

    started = []

    def go(src, dst, step):
        i = len(started)
        copy = pltpu.make_async_remote_copy(
            src_ref=src, dst_ref=dst, send_sem=send.at[i], recv_sem=recv.at[i],
            device_id=at(step), device_id_type=MESH,
        )
        copy.start()
        started.append(copy)
        return copy

    def rows_of(index, n):
        return pl.ds(pl.multiple_of(index * n, n), n)

    part = parting(width)
    for copy in ins:
        copy.wait()
    vals = vel[...].astype(F32)
    both = jnp.concatenate([vals, vals], 0)
    node_blocks = wide.shape[0]
    for b in range(node_blocks):
        wide[b] = both[:, b * width : (b + 1) * width]
    table[...] = to_parts(
        wide[...].reshape(node_blocks * ROWS, width).astype(BF16), part
    ).reshape(table.shape)
    for i in range(slots // PER):
        coefs[i].wait()
        for copy in coefs[i + AHEAD : i + AHEAD + 1]:
            copy.start()
        if i == len(coefs) - 1:
            for load in loads:
                load.start()

        def two(s, carry, i=i):
            q = i * PER + 2 * s
            term = pair_term(table, lambda j: struct[0, j], coef, q, NT)
            pair_rows[pl.ds(pl.multiple_of(q * ROWS, 2 * ROWS), 2 * ROWS), :] = term
            return carry

        lax.fori_loop(0, PER // 2, two, 0, unroll=PER // 2)

    terms_16 = []
    for r in range(ROWS):
        term = pair_rows[pl.ds(r, slots, stride=ROWS), :]
        high = term.astype(BF16)
        low = (term - high.astype(F32)).astype(BF16)
        terms_16.append(jnp.concatenate([high, low], 0))
    half_blocks = nx * chips
    place = lax.broadcasted_iota(jnp.int32, (half_blocks, slots), 0)
    block = (place % nx) * (chips * CORES) + place // nx * CORES
    slot = lax.broadcasted_iota(jnp.int32, (half_blocks, slots), 1)
    live = slot < count[0, 0]

    def block_sums(of_core, into):
        hit = jnp.where((panel_row[...] == block + of_core) & live, 1.0, 0.0).astype(BF16)
        hit = jnp.concatenate([hit, hit], 1)
        for r in range(ROWS):
            into[pl.ds(r, half_blocks, stride=ROWS), :] = lax.dot_general(
                hit, terms_16[r], NN, preferred_element_type=F32
            )

    block_sums(1 - core, other_half)
    pl.semaphore_wait(barrier, len(friends))
    copy = go(other_half, got_core, sibling)
    block_sums(core, own_half)
    copy.wait_recv()
    got_core[...] = own_half[...] + got_core[...]

    def block_at(step):
        return rows_of(chip_at(*step[1:3]) * nx + lax.rem(col + step[0], nx), ROWS)

    copies = {
        s: go(got_core.at[block_at(s)], got_all.at[k], s)
        for k, s in reversed(list(enumerate(to_owner)))
    }
    total = got_core[block_at((0, 0, 0, 0)), :]
    for k, s in enumerate(to_owner):
        copies[s].wait_recv()
        total = total + got_all[k]
    mixed = from_parts(total.astype(BF16).astype(F32), part)
    line[row] = jnp.concatenate([mixed[:, :size], mixed[:, size:]], 0).astype(BF16)

    def source(s):
        return row_at((-s[1], -s[2], s[3]))

    def send_out(ref, over):
        return {s: go(ref(row), ref(row), s) for s in over[::-1]}

    def came(piece, over):
        over = list(over)
        for s in over:
            piece[s].wait_recv()
        return [source(s) for s in over]

    def entries(r):
        both = line[r].astype(F32)
        return jnp.concatenate([both[:ROWS], both[ROWS:]], 1)

    split = press_rows * 5 // 8

    def products(rows):
        still, moving = 0.0, 0.0
        for r in rows:
            x = entries(r).astype(BF16)
            still += lax.dot_general(x, bem[r, :split], NT, preferred_element_type=F32)
            moving += lax.dot_general(bem[r, split:], x, NT, preferred_element_type=F32)
        return still, moving

    def plus(one, other):
        return one[0] + other[0], one[1] + other[1]

    piece = send_out(lambda r: line.at[r], in_col)
    for load in loads:
        load.wait()
    sums = products([row])
    groups = [list(group) for _, group in itertools.groupby(in_col, key=hops)]
    for group in groups[:-1]:
        sums = plus(sums, products(came(piece, group)))
    sums = jnp.concatenate([sums[0], sums[1].T], 1)
    for r in came(piece, groups[-1]):
        sums += lax.dot_general(
            entries(r).astype(BF16), bem[r], NT, preferred_element_type=F32
        )

    first = row * own
    blocks = chips * CORES
    owner = first // blocks == col
    here = lax.rem(first, blocks)
    same = jnp.concatenate([entries(here + u) for u in range(own)], 1)
    summed = sums + jnp.where(owner, same * self_term[...], 0.0)
    terms[col] = summed[:cases] + summed[cases:]

    copies = [go(terms.at[col], terms.at[col], (d, 0, 0, 0)) for d in xs]
    for copy in copies:
        copy.wait_recv()
    total = terms[0]
    for j in range(1, nx):
        total = total + terms[j]
    rounded = total.astype(BF16)
    press[...] = rounded
    tall = rounded.astype(F32)
    tall = jnp.concatenate([tall, tall], 0)
    tall = jnp.concatenate([tall[:, u * width : (u + 1) * width] for u in range(own)], 0)
    n_own = own * ROWS
    full[rows_of(row, n_own), :] = to_parts(tall.astype(BF16), part).astype(BF16)

    def full_at(r):
        return full.at[rows_of(r, n_own)]

    came(send_out(full_at, in_col), in_col)
    for copy in started:
        copy.wait_send()


def on_device(nx, nz, ny, velocity, pair_struct, pair_panel, pair_count, mortar_coef, bem_matrix, self_term):
    cases = velocity.shape[0]
    slots, panel_size, node_size = mortar_coef.shape
    node_blocks = velocity.shape[1] // (2 * node_size)
    width = 2 * panel_size
    press_rows = bem_matrix.shape[0]
    chips = nz * ny
    col_blocks = chips * CORES
    panel_blocks = nx * col_blocks
    smem = pl.BlockSpec(memory_space=pltpu.SMEM)
    vmem = pl.BlockSpec(memory_space=pltpu.VMEM)
    hbm = pl.BlockSpec(memory_space=pltpu.HBM)
    struct, panel, count = pair_struct[None, :], pair_panel[None, :], pair_count[None, :]

    sends = nx * chips + 2 * (col_blocks - 1) + nx - 1
    dma = pltpu.SemaphoreType.DMA
    pressure, full, coef = pl.pallas_call(
        functools.partial(field_kernel, nx, nz, ny),
        out_shape=(
            jax.ShapeDtypeStruct((cases, press_rows), BF16),
            jax.ShapeDtypeStruct((panel_blocks * ROWS, panel_size), BF16),
            jax.ShapeDtypeStruct(mortar_coef.shape, BF16),
        ),
        in_specs=[smem] + [hbm] * 6,
        out_specs=(vmem, vmem, vmem),
        scratch_shapes=[
            pltpu.SMEM((1, slots), jnp.int32),
            pltpu.SMEM((1, slots), jnp.int32),
            pltpu.VMEM((1, slots), jnp.int32),
            pltpu.VMEM(velocity.shape, BF16),
            pltpu.VMEM((col_blocks, press_rows, width), BF16),
            pltpu.VMEM((1, press_rows), F32),
            pltpu.VMEM((node_blocks, ROWS, 2 * node_size), F32),
            pltpu.VMEM((node_blocks, ROWS, node_size), F32),
            pltpu.VMEM((slots * ROWS, panel_size), F32),
            pltpu.VMEM((panel_blocks * ROWS // CORES, panel_size), F32),
            pltpu.VMEM((panel_blocks * ROWS // CORES, panel_size), F32),
            pltpu.VMEM((panel_blocks * ROWS // CORES, panel_size), F32),
            pltpu.VMEM((nx * chips - 1, ROWS, panel_size), F32),
            pltpu.VMEM((col_blocks, 2 * ROWS, panel_size), BF16),
            pltpu.VMEM((nx, cases, press_rows), F32),
            dma((5,)),
            dma((slots // PER,)),
            dma((col_blocks,)),
            dma((sends,)),
            dma((sends,)),
        ],
        compiler_params=pltpu.CompilerParams(
            collective_id=0, has_side_effects=True, vmem_limit_bytes=44 << 20
        ),
        cost_estimate=pl.CostEstimate(
            flops=2 * cases * bem_matrix.size,
            bytes_accessed=2 * bem_matrix.size,
            transcendentals=0,
        ),
        name="field",
    )(
        count,
        *[
            pltpu.with_memory_space_constraint(x, pltpu.HBM)
            for x in (struct, panel, velocity, mortar_coef, bem_matrix, self_term[None, :])
        ],
    )

    load, pressure = pl.pallas_call(
        backward_kernel,
        out_shape=(
            jax.ShapeDtypeStruct(velocity.shape, F32),
            jax.ShapeDtypeStruct((cases, press_rows), BF16),
        ),
        in_specs=[smem, smem, smem, vmem, vmem, vmem],
        out_specs=(vmem, vmem),
        scratch_shapes=[
            pltpu.VMEM((panel_blocks, ROWS, panel_size), F32),
            pltpu.VMEM((node_blocks, ROWS, node_size), F32),
        ],
        compiler_params=pltpu.CompilerParams(vmem_limit_bytes=24 << 20),
        cost_estimate=pl.CostEstimate(
            flops=2 * ROWS * mortar_coef.size,
            bytes_accessed=2 * mortar_coef.size,
            transcendentals=0,
        ),
        name="mortar_backward",
    )(struct, panel, count, pressure, full, coef)
    return pressure, load


def solution(mesh):
    nx = mesh.shape["col"]
    chips = mesh.shape["row"] // CORES
    nz = nx if chips % nx == 0 else 1
    placed = (
        P(None, ("col", "row")),
        P(("col", "row")),
        P(("col", "row")),
        P(("col", "row")),
        P(("col", "row"), None, None),
        P("row", "col"),
        P("row"),
    )
    return jax.shard_map(
        functools.partial(on_device, nx, nz, chips // nz),
        mesh=mesh,
        in_specs=placed,
        out_specs=(P(None, "row"), P(None, ("col", "row"))),
        check_vma=False,
    )
```
